512 devices in a mesh: wide: 64 (over z_lo, y, core), mid: 4 (over x), narrow: 2 (over z_hi).
Axes of the slice: x: 4, y: 4, z: 16 (z_hi: 2, z_lo: 8; z = z_hi * 8 + z_lo), core: 2. Of those that a mesh axis runs over, the one named last changes fastest.
Arguments:
- amplitudes: float32 [2, 134217728], P(None, ('wide', 'mid', 'narrow')), may hold values from -6 to 6
- gates: float32 [3, 2, 128, 128], replicated, may hold values from -0.375 to 0.375
- qubit_sets: int32 [3, 7], replicated, may hold values from 0 to 17, as said below
Outputs:
- evolved: float32 [2, 134217728], P(None, ('wide', 'mid', 'narrow'))
The draws below stay inside these ranges and needn't reach their ends.
Inputs may be any that keep to these rules, and one draw needn't show every extreme that they name: `qubit_sets`: in each row the last entry is 17 and the other entries are distinct qubits among 0 to 6.
All inputs are finite; a program needn't handle non-finite values.
Results may differ from the reference program's by a relative error of at most 0.011.
Values may be sent and summed in bfloat16 or wider, within the bound.
A program may use at most 64 MiB of HBM per device.

```python
import jax
import jax.numpy as jnp
from jax import lax

LOCAL_QUBITS = 18
GATE_QUBITS = 7
BLOCK = 256
LAYERS = 3
SPAN = 262144
HALF = 131072
GATE_DIM = 128
AMPS = 134217728
N_WIDE = 64
N_MID = 4
N_NARROW = 2
DEVICES = 512


def draw_qubit_sets(key, part):
    key = jax.random.fold_in(key, 7)
    row_list = []
    for layer_index in range(LAYERS):
        shuffled = jax.random.permutation(jax.random.fold_in(key, layer_index), 7).astype(jnp.int32)
        topmost = jnp.full((1,), LOCAL_QUBITS - 1, jnp.int32)
        row_list.append(jnp.concatenate([shuffled[:GATE_QUBITS - 1], topmost]))
    return jnp.stack(row_list).astype(jnp.int32)


def levels(rng, extent, split, smallest, largest):
    def one(dim, shards_of):
        heights = jax.random.uniform(jax.random.fold_in(jax.random.fold_in(rng, 6), dim), (shards_of,), jnp.float32, smallest / len(split), largest / len(split))
        return jnp.repeat(jnp.exp(heights), extent[dim] // shards_of).reshape((-1,) + (1,) * (len(extent) - dim - 1))

    factor_of = one(*split[0])
    for cut in split[1:]:
        factor_of = factor_of * one(*cut)
    return factor_of


def noise(key, shape, scale, reach, split=(), kind=jnp.bfloat16):
    values = scale * jax.random.normal(key, shape, jnp.float32)
    if split:
        values = values * levels(key, shape, split, -0.22, 0.18)
    return jnp.clip(values, -reach, reach).astype(kind)


def setup_inputs(seed: int = 0) -> dict:
    key_list = jax.random.split(jax.random.key(seed), 4)
    amplitudes = noise(key_list[0], (2, AMPS), 1.0, 6.0, ((1, 512),), jnp.float32)
    gates = noise(key_list[1], (LAYERS, 2, GATE_DIM, GATE_DIM), (2 * GATE_DIM) ** -0.5, 0.375, (), jnp.float32)
    qubit_sets = draw_qubit_sets(jax.random.fold_in(key_list[3], 71), 0)
    return dict(amplitudes=amplitudes, gates=gates, qubit_sets=qubit_sets)


def full_gate(matrix, qubits, local_bits):
    places = jnp.where(qubits == local_bits - 1, 7, qubits).astype(jnp.int32)
    spare = (28 - jnp.sum(places)).astype(jnp.int32)
    cells = jnp.arange(256, dtype=jnp.int32)
    gate_index = jnp.zeros((256,), jnp.int32)
    for bit_pos in range(qubits.shape[0]):
        gate_index = gate_index + (((cells >> places[bit_pos]) & 1) << bit_pos)
    select = (gate_index[:, None] == jnp.arange(128, dtype=jnp.int32)[None, :]).astype(jnp.float32)
    spare_bit = (cells >> spare) & 1
    same = (spare_bit[:, None] == spare_bit[None, :]).astype(jnp.float32)
    spread = jnp.einsum("ak,skj,bj->sab", select, matrix, select, precision=lax.Precision.HIGHEST)
    return spread * same[None]


def block_code(values_in):
    shaped = values_in.reshape(values_in.shape[:-1] + (values_in.shape[-1] // BLOCK, BLOCK))
    magnitude = jnp.max(jnp.abs(shaped), axis=(0, shaped.ndim - 1)) + 1e-6
    scales = magnitude.astype(jnp.bfloat16).astype(jnp.float32)
    coded = (shaped / scales[None, ..., None]).astype(jnp.bfloat16).astype(jnp.float32)
    return (coded * scales[None, ..., None]).reshape(values_in.shape)


def exchange_global(amplitudes, below):
    view = amplitudes.reshape(2, -1, 2, below, 2, HALF)
    keep_low = view[:, :, 0, :, 0]
    keep_high = view[:, :, 1, :, 1]
    moved_up = block_code(view[:, :, 1, :, 0])
    moved_down = block_code(view[:, :, 0, :, 1])
    upper_group = jnp.stack([keep_low, moved_up], axis=3)
    lower_group = jnp.stack([moved_down, keep_high], axis=3)
    return jnp.stack([upper_group, lower_group], axis=2).reshape(2, -1)


def apply_gate(block_in, matrix):
    real_part = jnp.einsum("bk,rk->br", block_in[0], matrix[0], precision=lax.Precision.HIGHEST) - jnp.einsum("bk,rk->br", block_in[1], matrix[1], precision=lax.Precision.HIGHEST)
    imag_part = jnp.einsum("bk,rk->br", block_in[0], matrix[1], precision=lax.Precision.HIGHEST) + jnp.einsum("bk,rk->br", block_in[1], matrix[0], precision=lax.Precision.HIGHEST)
    return jnp.stack([real_part, imag_part])


def reference(amplitudes, gates, qubit_sets):
    belows = [N_WIDE // 2 * N_MID * N_NARROW, N_MID * N_NARROW, 1]
    current = amplitudes
    for layer_index in range(LAYERS):
        current = exchange_global(current, belows[layer_index])
        matrix = full_gate(gates[layer_index], qubit_sets[layer_index], LOCAL_QUBITS)

        def one_span(span_data):
            lower = span_data[:, :HALF].reshape(2, -1, 128)
            upper = span_data[:, HALF:].reshape(2, -1, 128)
            block_in = jnp.concatenate([lower, upper], axis=-1)
            result = apply_gate(block_in, matrix)
            return jnp.concatenate([result[:, :, :128].reshape(2, -1), result[:, :, 128:].reshape(2, -1)], axis=1)

        spans = jnp.transpose(current.reshape(2, DEVICES, SPAN), (1, 0, 2))
        spans = lax.map(one_span, spans)
        current = jnp.transpose(spans, (1, 0, 2)).reshape(2, -1)
    return current
```

```python
import functools

import jax
import jax.numpy as jnp
from jax import lax
from jax.experimental import pallas as pl
from jax.experimental.pallas import tpu as pltpu
from jax.sharding import PartitionSpec as P

LAYERS = 3
ROWS = 1024
CHUNKS = 8
STEP = ROWS // CHUNKS
PAIRS = STEP // 2


def scaled(parts):
    peak = jnp.maximum(
        jnp.maximum(jnp.abs(parts[0]), jnp.abs(parts[1])),
        jnp.maximum(jnp.abs(parts[2]), jnp.abs(parts[3])),
    )
    magnitude = jnp.max(peak, axis=1, keepdims=True) + 1e-06
    scale = magnitude.astype(jnp.bfloat16).astype(jnp.float32)
    inverse = 1.0 / scale
    coded = [(part * inverse).astype(jnp.bfloat16).astype(jnp.float32) for part in parts]
    return [(part * scale).astype(jnp.bfloat16) for part in coded]


def put(ref, chunk, parts):
    ref[chunk, :PAIRS, :128] = parts[0]
    ref[chunk, :PAIRS, 128:] = parts[1]
    ref[chunk, PAIRS:, :128] = parts[2]
    ref[chunk, PAIRS:, 128:] = parts[3]


def quarters(tile):
    return [tile[:PAIRS, :128], tile[:PAIRS, 128:], tile[PAIRS:, :128], tile[PAIRS:, 128:]]


def spread_gate(layer, own, following, gates_ref, sets_ref, weights):
    cells = lax.broadcasted_iota(jnp.int32, (256, 128), 0)
    wanted = lax.broadcasted_iota(jnp.int32, (256, 128), 1)
    cell_in = lax.broadcasted_iota(jnp.int32, (256, 256), 0)
    cell_out = lax.broadcasted_iota(jnp.int32, (256, 256), 1)
    gate_index = jnp.zeros((256, 128), jnp.int32)
    spare = jnp.int32(28)
    for bit_pos in range(7):
        qubit = sets_ref[layer, bit_pos]
        place = jnp.where(qubit == 17, 7, qubit)
        spare = spare - place
        gate_index = gate_index + (((cells >> place) & 1) << bit_pos)
    select = (gate_index == wanted).astype(jnp.float32).astype(jnp.bfloat16)
    same = ((cell_in >> spare) & 1) == ((cell_out >> spare) & 1)
    last_dims = (((1,), (1,)), ((), ()))
    spreads = []
    for part in range(2):
        matrix = gates_ref[layer, part].astype(jnp.bfloat16)
        half_way = lax.dot_general(select, matrix, last_dims, preferred_element_type=jnp.float32)
        whole = lax.dot_general(
            half_way.astype(jnp.bfloat16), select, last_dims, preferred_element_type=jnp.float32
        )
        spreads.append(jnp.where(same, whole, 0.0))
    real, imag = spreads
    for u_in in range(2):
        row = pl.multiple_of(lax.rem(u_in + own + 1, 2) * 256, 256)
        for u_out in range(2):
            if following is None:
                column = u_out * 256
            else:
                column = pl.multiple_of(lax.rem(u_out + following + 1, 2) * 256, 256)
            re = real[u_in * 128 : u_in * 128 + 128, u_out * 128 : u_out * 128 + 128].astype(jnp.bfloat16)
            im = imag[u_in * 128 : u_in * 128 + 128, u_out * 128 : u_out * 128 + 128].astype(jnp.bfloat16)
            weights[layer, pl.ds(row, 128), pl.ds(column, 128)] = re
            weights[layer, pl.ds(row, 128), pl.ds(column + 128, 128)] = im
            weights[layer, pl.ds(row + 128, 128), pl.ds(column, 128)] = -im
            weights[layer, pl.ds(row + 128, 128), pl.ds(column + 128, 128)] = re


def kernel(
    sets_ref,
    gates_ref,
    x_ref,
    out_ref,
    x_v,
    out_v,
    weights,
    send,
    recv,
    kept,
    load_sem,
    rest_sem,
    send_sem,
    recv_sem,
    store_sem,
):
    wide = lax.axis_index("wide")
    narrow = lax.axis_index("narrow")
    n_wide = lax.axis_size("wide")
    own = [wide // (n_wide // 2), lax.rem(wide, 2), narrow]
    partners = [
        {"wide": lax.rem(wide + n_wide // 2, n_wide)},
        {"wide": wide + 1 - 2 * own[1]},
        {"narrow": 1 - narrow},
    ]

    barrier = pltpu.get_barrier_semaphore()
    for partner in partners:
        pl.semaphore_signal(barrier, inc=1, device_id=partner, device_id_type=pl.DeviceIdType.MESH)

    away = pl.multiple_of((1 - own[0]) * 2 * ROWS, 2 * ROWS)
    home = pl.multiple_of(own[0] * 2 * ROWS, 2 * ROWS)

    def load(chunk):
        rows = pl.ds(away + chunk * 2 * STEP, 2 * STEP)
        return pltpu.make_async_copy(x_ref.at[rows], x_v.at[rows], load_sem.at[chunk])

    rest = pltpu.make_async_copy(x_ref.at[pl.ds(home, 2 * ROWS)], x_v.at[pl.ds(home, 2 * ROWS)], rest_sem)

    def exchange(layer, chunk):
        return pltpu.make_async_remote_copy(
            src_ref=send.at[layer, chunk],
            dst_ref=recv.at[layer, chunk],
            send_sem=send_sem.at[layer, chunk],
            recv_sem=recv_sem.at[layer, chunk],
            device_id=partners[layer],
            device_id_type=pl.DeviceIdType.MESH,
        )

    def store(half, chunk):
        rows = pl.ds(pl.multiple_of(half * 2 * ROWS + chunk * 2 * STEP, 2 * STEP), 2 * STEP)
        return pltpu.make_async_copy(out_v.at[rows], out_ref.at[rows], store_sem.at[half, chunk])

    def read(base, chunk):
        start = base + chunk * 2 * STEP
        return [x_v[pl.ds(start + part, PAIRS, stride=4), :] for part in range(4)]

    for chunk in range(CHUNKS):
        load(chunk).start()
    rest.start()

    pl.semaphore_wait(barrier, 3)

    @pl.loop(0, CHUNKS)
    def _(chunk):
        load(chunk).wait()
        put(send.at[0], chunk, scaled(read(away, chunk)))
        exchange(0, chunk).start()

    spread_gate(0, own[0], own[1], gates_ref, sets_ref, weights)
    rest.wait()

    @pl.loop(0, CHUNKS)
    def _(chunk):
        put(kept.at[0], chunk, [part.astype(jnp.bfloat16) for part in read(home, chunk)])

    spread_gate(1, own[1], own[2], gates_ref, sets_ref, weights)
    spread_gate(2, own[2], None, gates_ref, sets_ref, weights)

    def gate(layer, chunk):
        exchange(layer, chunk).wait_recv()
        block = jnp.concatenate([recv[layer, chunk], kept[layer, chunk]], axis=1)
        return jnp.dot(block, weights[layer], preferred_element_type=jnp.float32)

    def advance(layer, chunk):
        result = gate(layer, chunk)
        put(send.at[layer + 1], chunk, scaled(quarters(result[:, :256])))
        exchange(layer + 1, chunk).start()
        kept[layer + 1, chunk] = result[:, 256:].astype(jnp.bfloat16)

    advance(0, 0)

    @pl.loop(1, CHUNKS)
    def _(chunk):
        advance(0, chunk)
        advance(1, chunk - 1)

    advance(1, CHUNKS - 1)

    @pl.loop(0, CHUNKS)
    def _(chunk):
        result = gate(2, chunk)
        for half in range(2):
            start = half * 2 * ROWS + chunk * 2 * STEP
            for part, value in enumerate(quarters(result[:, half * 256 : half * 256 + 256])):
                out_v[pl.ds(start + part, PAIRS, stride=4), :] = value
            store(half, chunk).start()

    @pl.loop(0, CHUNKS)
    def _(chunk):
        for layer in range(LAYERS):
            exchange(layer, chunk).wait_send()
        for half in range(2):
            store(half, chunk).wait()


def on_device(amplitudes, gates, qubit_sets):
    rows = amplitudes.reshape(2, 2 * ROWS, 128).transpose(1, 0, 2).reshape(4 * ROWS, 128)
    out = pl.pallas_call(
        kernel,
        out_shape=jax.ShapeDtypeStruct((4 * ROWS, 128), jnp.float32),
        in_specs=[
            pl.BlockSpec(memory_space=pltpu.SMEM),
            pl.BlockSpec(memory_space=pltpu.VMEM),
            pl.BlockSpec(memory_space=pl.ANY),
        ],
        out_specs=pl.BlockSpec(memory_space=pl.ANY),
        scratch_shapes=[
            pltpu.VMEM((4 * ROWS, 128), jnp.float32),
            pltpu.VMEM((4 * ROWS, 128), jnp.float32),
            pltpu.VMEM((LAYERS, 512, 512), jnp.bfloat16),
            pltpu.VMEM((LAYERS, CHUNKS, STEP, 256), jnp.bfloat16),
            pltpu.VMEM((LAYERS, CHUNKS, STEP, 256), jnp.bfloat16),
            pltpu.VMEM((LAYERS, CHUNKS, STEP, 256), jnp.bfloat16),
            pltpu.SemaphoreType.DMA((CHUNKS,)),
            pltpu.SemaphoreType.DMA,
            pltpu.SemaphoreType.DMA((LAYERS, CHUNKS)),
            pltpu.SemaphoreType.DMA((LAYERS, CHUNKS)),
            pltpu.SemaphoreType.DMA((2, CHUNKS)),
        ],
        compiler_params=pltpu.CompilerParams(
            collective_id=0, has_side_effects=True, vmem_limit_bytes=40 * 1024 * 1024
        ),
        name="layers",
    )(qubit_sets, gates, rows)
    return out.reshape(2 * ROWS, 2, 128).transpose(1, 0, 2).reshape(2, 2 * ROWS * 128)


def solution(mesh):
    in_specs = (P(None, ("wide", "mid", "narrow")), P(), P())
    out_specs = P(None, ("wide", "mid", "narrow"))
    return jax.shard_map(
        on_device, mesh=mesh, in_specs=in_specs, out_specs=out_specs, check_vma=False
    )
```

```python
import functools

import jax
import jax.numpy as jnp
from jax import lax
from jax.experimental import pallas as pl
from jax.experimental.pallas import tpu as pltpu
from jax.sharding import PartitionSpec as P

LAYERS = 3
ROWS = 1024
CHUNKS = 8
STEP = ROWS // CHUNKS
PAIRS = STEP // 2
EARLY = CHUNKS // 2


def scaled(parts):
    peak = jnp.maximum(
        jnp.maximum(jnp.abs(parts[0]), jnp.abs(parts[1])),
        jnp.maximum(jnp.abs(parts[2]), jnp.abs(parts[3])),
    )
    magnitude = jnp.max(peak, axis=1, keepdims=True) + 1e-06
    scale = magnitude.astype(jnp.bfloat16).astype(jnp.float32)
    inverse = 1.0 / scale
    coded = [(part * inverse).astype(jnp.bfloat16).astype(jnp.float32) for part in parts]
    return [(part * scale).astype(jnp.bfloat16) for part in coded]


def put(ref, chunk, parts):
    ref[chunk, :PAIRS, :128] = parts[0]
    ref[chunk, :PAIRS, 128:] = parts[1]
    ref[chunk, PAIRS:, :128] = parts[2]
    ref[chunk, PAIRS:, 128:] = parts[3]


def quarters(tile):
    return [tile[:PAIRS, :128], tile[:PAIRS, 128:], tile[PAIRS:, :128], tile[PAIRS:, 128:]]


def spread_gate(layer, own, following, gates_ref, sets_ref, weights):
    cells = lax.broadcasted_iota(jnp.int32, (256, 128), 0)
    wanted = lax.broadcasted_iota(jnp.int32, (256, 128), 1)
    cell_in = lax.broadcasted_iota(jnp.int32, (256, 256), 0)
    cell_out = lax.broadcasted_iota(jnp.int32, (256, 256), 1)
    gate_index = jnp.zeros((256, 128), jnp.int32)
    spare = jnp.int32(28)
    for bit_pos in range(7):
        qubit = sets_ref[layer, bit_pos]
        place = jnp.where(qubit == 17, 7, qubit)
        spare = spare - place
        gate_index = gate_index + (((cells >> place) & 1) << bit_pos)
    select = (gate_index == wanted).astype(jnp.float32).astype(jnp.bfloat16)
    same = ((cell_in >> spare) & 1) == ((cell_out >> spare) & 1)
    last_dims = (((1,), (1,)), ((), ()))
    spreads = []
    for part in range(2):
        matrix = gates_ref[layer, part].astype(jnp.bfloat16)
        half_way = lax.dot_general(select, matrix, last_dims, preferred_element_type=jnp.float32)
        whole = lax.dot_general(
            half_way.astype(jnp.bfloat16), select, last_dims, preferred_element_type=jnp.float32
        )
        spreads.append(jnp.where(same, whole, 0.0))
    real, imag = spreads
    for u_in in range(2):
        row = pl.multiple_of(lax.rem(u_in + own + 1, 2) * 256, 256)
        for u_out in range(2):
            if following is None:
                column = u_out * 256
            else:
                column = pl.multiple_of(lax.rem(u_out + following + 1, 2) * 256, 256)
            re = real[u_in * 128 : u_in * 128 + 128, u_out * 128 : u_out * 128 + 128].astype(jnp.bfloat16)
            im = imag[u_in * 128 : u_in * 128 + 128, u_out * 128 : u_out * 128 + 128].astype(jnp.bfloat16)
            weights[layer, pl.ds(row, 128), pl.ds(column, 128)] = re
            weights[layer, pl.ds(row, 128), pl.ds(column + 128, 128)] = im
            weights[layer, pl.ds(row + 128, 128), pl.ds(column, 128)] = -im
            weights[layer, pl.ds(row + 128, 128), pl.ds(column + 128, 128)] = re


def kernel(
    sets_hbm,
    gates_hbm,
    x_ref,
    out_ref,
    sets_ref,
    gates_ref,
    x_v,
    out_v,
    weights,
    send,
    recv,
    kept,
    load_sem,
    rest_sem,
    send_sem,
    recv_sem,
    store_sem,
):
    wide = lax.axis_index("wide")
    narrow = lax.axis_index("narrow")
    n_wide = lax.axis_size("wide")
    own = [wide // (n_wide // 2), lax.rem(wide, 2), narrow]
    across = lax.rem(wide + n_wide // 2, n_wide)
    partner_f = {"wide": across}
    partner_g = {"wide": across, "narrow": 1 - narrow}
    core = {"wide": wide + 1 - 2 * own[1]}

    barrier = pltpu.get_barrier_semaphore()
    for partner in (partner_f, partner_g, core):
        pl.semaphore_signal(barrier, inc=1, device_id=partner, device_id_type=pl.DeviceIdType.MESH)

    away = pl.multiple_of((1 - own[0]) * 2 * ROWS, 2 * ROWS)
    home = pl.multiple_of(own[0] * 2 * ROWS, 2 * ROWS)

    def load(chunk):
        rows = pl.ds(away + chunk * 2 * STEP, 2 * STEP)
        return pltpu.make_async_copy(x_ref.at[rows], x_v.at[rows], load_sem.at[chunk])

    rest = [
        pltpu.make_async_copy(x_ref.at[pl.ds(home, 2 * ROWS)], x_v.at[pl.ds(home, 2 * ROWS)], rest_sem.at[0]),
        pltpu.make_async_copy(gates_hbm, gates_ref, rest_sem.at[1]),
        pltpu.make_async_copy(sets_hbm, sets_ref, rest_sem.at[2]),
    ]

    def exchange(stage, chunk, partner):
        source = send.at[stage, chunk] if stage < 3 else recv.at[2, chunk]
        return pltpu.make_async_remote_copy(
            src_ref=source,
            dst_ref=recv.at[stage, chunk],
            send_sem=send_sem.at[stage, chunk],
            recv_sem=recv_sem.at[stage, chunk],
            device_id=partner,
            device_id_type=pl.DeviceIdType.MESH,
        )

    def store(half, chunk):
        rows = pl.ds(pl.multiple_of(half * 2 * ROWS + chunk * 2 * STEP, 2 * STEP), 2 * STEP)
        return pltpu.make_async_copy(out_v.at[rows], out_ref.at[rows], store_sem.at[half, chunk])

    def read(base, chunk):
        start = base + chunk * 2 * STEP
        return [x_v[pl.ds(start + part, PAIRS, stride=4), :] for part in range(4)]

    for chunk in range(CHUNKS):
        load(chunk).start()
    for copy in rest:
        copy.start()

    def first(chunk):
        load(chunk).wait()
        put(send.at[0], chunk, scaled(read(away, chunk)))

    first(0)
    pl.semaphore_wait(barrier, 3)
    exchange(0, 0, partner_f).start()

    @pl.loop(1, CHUNKS)
    def _(chunk):
        first(chunk)
        exchange(0, chunk, partner_f).start()

    for copy in rest:
        copy.wait()
    spread_gate(0, own[0], own[1], gates_ref, sets_ref, weights)

    @pl.loop(0, CHUNKS)
    def _(chunk):
        put(kept.at[0], chunk, [part.astype(jnp.bfloat16) for part in read(home, chunk)])

    spread_gate(1, own[1], own[2], gates_ref, sets_ref, weights)
    spread_gate(2, own[2], None, gates_ref, sets_ref, weights)

    def gate(layer, stage, chunk):
        exchange(stage, chunk, core).wait_recv()
        block = jnp.concatenate([recv[stage, chunk], kept[layer, chunk]], axis=1)
        return jnp.dot(block, weights[layer], preferred_element_type=jnp.float32)

    def advance(layer, chunk, partner):
        result = gate(layer, layer, chunk)
        put(send.at[layer + 1], chunk, scaled(quarters(result[:, :256])))
        exchange(layer + 1, chunk, partner).start()
        kept[layer + 1, chunk] = result[:, 256:].astype(jnp.bfloat16)

    advance(0, 0, core)

    @pl.loop(1, EARLY + 1)
    def _(chunk):
        advance(0, chunk, core)
        advance(1, chunk - 1, partner_g)

    @pl.loop(EARLY + 1, CHUNKS)
    def _(chunk):
        advance(0, chunk, core)
        advance(1, chunk - 1, partner_f)

    advance(1, CHUNKS - 1, partner_f)

    @pl.loop(0, EARLY)
    def _(chunk):
        exchange(2, chunk, core).wait_recv()
        exchange(3, chunk, partner_f).start()

    @pl.loop(EARLY, CHUNKS)
    def _(chunk):
        exchange(2, chunk, core).wait_recv()
        exchange(3, chunk, partner_g).start()

    @pl.loop(0, CHUNKS)
    def _(chunk):
        result = gate(2, 3, chunk)
        for half in range(2):
            start = half * 2 * ROWS + chunk * 2 * STEP
            for part, value in enumerate(quarters(result[:, half * 256 : half * 256 + 256])):
                out_v[pl.ds(start + part, PAIRS, stride=4), :] = value
            store(half, chunk).start()

    @pl.loop(0, CHUNKS)
    def _(chunk):
        for stage in range(4):
            exchange(stage, chunk, core).wait_send()
        for half in range(2):
            store(half, chunk).wait()


def on_device(amplitudes, gates, qubit_sets):
    rows = amplitudes.reshape(2, 2 * ROWS, 128).transpose(1, 0, 2).reshape(4 * ROWS, 128)
    out = pl.pallas_call(
        kernel,
        out_shape=jax.ShapeDtypeStruct((4 * ROWS, 128), jnp.float32),
        in_specs=[
            pl.BlockSpec(memory_space=pl.ANY),
            pl.BlockSpec(memory_space=pl.ANY),
            pl.BlockSpec(memory_space=pl.ANY),
        ],
        out_specs=pl.BlockSpec(memory_space=pl.ANY),
        scratch_shapes=[
            pltpu.SMEM((LAYERS, 7), jnp.int32),
            pltpu.VMEM((LAYERS, 2, 128, 128), jnp.float32),
            pltpu.VMEM((4 * ROWS, 128), jnp.float32),
            pltpu.VMEM((4 * ROWS, 128), jnp.float32),
            pltpu.VMEM((LAYERS, 512, 512), jnp.bfloat16),
            pltpu.VMEM((3, CHUNKS, STEP, 256), jnp.bfloat16),
            pltpu.VMEM((4, CHUNKS, STEP, 256), jnp.bfloat16),
            pltpu.VMEM((3, CHUNKS, STEP, 256), jnp.bfloat16),
            pltpu.SemaphoreType.DMA((CHUNKS,)),
            pltpu.SemaphoreType.DMA((3,)),
            pltpu.SemaphoreType.DMA((4, CHUNKS)),
            pltpu.SemaphoreType.DMA((4, CHUNKS)),
            pltpu.SemaphoreType.DMA((2, CHUNKS)),
        ],
        compiler_params=pltpu.CompilerParams(
            collective_id=0, has_side_effects=True, vmem_limit_bytes=60 * 1024 * 1024
        ),
        name="layers",
    )(qubit_sets, gates, rows)
    return out.reshape(2 * ROWS, 2, 128).transpose(1, 0, 2).reshape(2, 2 * ROWS * 128)


def solution(mesh):
    in_specs = (P(None, ("wide", "mid", "narrow")), P(), P())
    out_specs = P(None, ("wide", "mid", "narrow"))
    return jax.shard_map(
        on_device, mesh=mesh, in_specs=in_specs, out_specs=out_specs, check_vma=False
    )
```

```python
import functools

import jax
import jax.numpy as jnp
from jax import lax
from jax.experimental import pallas as pl
from jax.experimental.pallas import tpu as pltpu
from jax.sharding import PartitionSpec as P

LAYERS = 3
ROWS = 1024
CHUNKS = 8
STEP = ROWS // CHUNKS
PAIRS = STEP // 2
EARLY = CHUNKS // 2


def scaled(parts):
    peak = jnp.maximum(
        jnp.maximum(jnp.abs(parts[0]), jnp.abs(parts[1])),
        jnp.maximum(jnp.abs(parts[2]), jnp.abs(parts[3])),
    )
    magnitude = jnp.max(peak, axis=1, keepdims=True) + 1e-06
    scale = magnitude.astype(jnp.bfloat16).astype(jnp.float32)
    inverse = 1.0 / scale
    coded = [(part * inverse).astype(jnp.bfloat16).astype(jnp.float32) for part in parts]
    return [(part * scale).astype(jnp.bfloat16) for part in coded]


def put(ref, chunk, parts):
    ref[chunk, :PAIRS, :128] = parts[0]
    ref[chunk, :PAIRS, 128:] = parts[1]
    ref[chunk, PAIRS:, :128] = parts[2]
    ref[chunk, PAIRS:, 128:] = parts[3]


def quarters(tile):
    return [tile[:PAIRS, :128], tile[:PAIRS, 128:], tile[PAIRS:, :128], tile[PAIRS:, 128:]]


def spread_gate(layer, own, following, gates_ref, sets_ref, weights):
    cells = lax.broadcasted_iota(jnp.int32, (256, 128), 0)
    wanted = lax.broadcasted_iota(jnp.int32, (256, 128), 1)
    cell_in = lax.broadcasted_iota(jnp.int32, (256, 256), 0)
    cell_out = lax.broadcasted_iota(jnp.int32, (256, 256), 1)
    gate_index = jnp.zeros((256, 128), jnp.int32)
    spare = jnp.int32(28)
    for bit_pos in range(7):
        qubit = sets_ref[layer, bit_pos]
        place = jnp.where(qubit == 17, 7, qubit)
        spare = spare - place
        gate_index = gate_index + (((cells >> place) & 1) << bit_pos)
    select = (gate_index == wanted).astype(jnp.float32).astype(jnp.bfloat16)
    same = ((cell_in >> spare) & 1) == ((cell_out >> spare) & 1)
    last_dims = (((1,), (1,)), ((), ()))
    spreads = []
    for part in range(2):
        matrix = gates_ref[layer, part].astype(jnp.bfloat16)
        half_way = lax.dot_general(select, matrix, last_dims, preferred_element_type=jnp.float32)
        whole = lax.dot_general(
            half_way.astype(jnp.bfloat16), select, last_dims, preferred_element_type=jnp.float32
        )
        spreads.append(jnp.where(same, whole, 0.0))
    real, imag = spreads
    for u_in in range(2):
        row = pl.multiple_of(lax.rem(u_in + own + 1, 2) * 256, 256)
        for u_out in range(2):
            if following is None:
                column = u_out * 256
            else:
                column = pl.multiple_of(lax.rem(u_out + following + 1, 2) * 256, 256)
            re = real[u_in * 128 : u_in * 128 + 128, u_out * 128 : u_out * 128 + 128].astype(jnp.bfloat16)
            im = imag[u_in * 128 : u_in * 128 + 128, u_out * 128 : u_out * 128 + 128].astype(jnp.bfloat16)
            weights[layer, pl.ds(row, 128), pl.ds(column, 128)] = re
            weights[layer, pl.ds(row, 128), pl.ds(column + 128, 128)] = im
            weights[layer, pl.ds(row + 128, 128), pl.ds(column, 128)] = -im
            weights[layer, pl.ds(row + 128, 128), pl.ds(column + 128, 128)] = re


def kernel(
    sets_hbm,
    gates_hbm,
    x_ref,
    out_ref,
    sets_ref,
    gates_ref,
    x_v,
    out_v,
    weights,
    send,
    recv,
    kept,
    load_sem,
    rest_sem,
    send_sem,
    recv_sem,
    store_sem,
):
    wide = lax.axis_index("wide")
    narrow = lax.axis_index("narrow")
    n_wide = lax.axis_size("wide")
    own = [wide // (n_wide // 2), lax.rem(wide, 2), narrow]
    across = lax.rem(wide + n_wide // 2, n_wide)
    partner_f = {"wide": across}
    partner_g = {"wide": across, "narrow": 1 - narrow}
    core = {"wide": wide + 1 - 2 * own[1]}

    barrier = pltpu.get_barrier_semaphore()
    for partner in (partner_f, partner_g, core):
        pl.semaphore_signal(barrier, inc=1, device_id=partner, device_id_type=pl.DeviceIdType.MESH)

    away = pl.multiple_of((1 - own[0]) * 2 * ROWS, 2 * ROWS)
    home = pl.multiple_of(own[0] * 2 * ROWS, 2 * ROWS)

    def load(chunk):
        rows = pl.ds(away + chunk * 2 * STEP, 2 * STEP)
        return pltpu.make_async_copy(x_ref.at[rows], x_v.at[rows], load_sem.at[chunk])

    rest = [
        pltpu.make_async_copy(x_ref.at[pl.ds(home, 2 * ROWS)], x_v.at[pl.ds(home, 2 * ROWS)], rest_sem.at[0]),
        pltpu.make_async_copy(gates_hbm, gates_ref, rest_sem.at[1]),
        pltpu.make_async_copy(sets_hbm, sets_ref, rest_sem.at[2]),
    ]

    def exchange(stage, chunk, partner):
        source = send.at[stage, chunk] if stage < 3 else recv.at[2, chunk]
        return pltpu.make_async_remote_copy(
            src_ref=source,
            dst_ref=recv.at[stage, chunk],
            send_sem=send_sem.at[stage, chunk],
            recv_sem=recv_sem.at[stage, chunk],
            device_id=partner,
            device_id_type=pl.DeviceIdType.MESH,
        )

    def store(half, chunk):
        rows = pl.ds(pl.multiple_of(half * 2 * ROWS + chunk * 2 * STEP, 2 * STEP), 2 * STEP)
        return pltpu.make_async_copy(out_v.at[rows], out_ref.at[rows], store_sem.at[half, chunk])

    def read(base, chunk):
        start = base + chunk * 2 * STEP
        return [x_v[pl.ds(start + part, PAIRS, stride=4), :] for part in range(4)]

    for chunk in range(CHUNKS):
        load(chunk).start()
    for copy in rest:
        copy.start()

    def send_first():
        @pl.loop(0, CHUNKS)
        def _(chunk):
            load(chunk).wait()
            put(send.at[0], chunk, scaled(read(away, chunk)))
            exchange(0, chunk, partner_f).start()

    def prepare():
        for copy in rest:
            copy.wait()
        spread_gate(0, own[0], own[1], gates_ref, sets_ref, weights)

        @pl.loop(0, CHUNKS)
        def _(chunk):
            put(kept.at[0], chunk, [part.astype(jnp.bfloat16) for part in read(home, chunk)])

        spread_gate(1, own[1], own[2], gates_ref, sets_ref, weights)
        spread_gate(2, own[2], None, gates_ref, sets_ref, weights)
        exchange(0, 0, core).wait_recv()

    pl.semaphore_wait(barrier, 3)
    send_first()
    prepare()

    holds = lax.rem(wide // (n_wide // 8), 8) == 7
    held = jnp.where(holds, 1, 0)

    def gate(layer, stage, chunk):
        block = jnp.concatenate([recv[stage, chunk], kept[layer, chunk]], axis=1)
        return jnp.dot(block, weights[layer], preferred_element_type=jnp.float32)

    def advance(layer, chunk, partner, arrived=False, hold=False):
        if not arrived:
            exchange(layer, chunk, core).wait_recv()
        result = gate(layer, layer, chunk)
        put(send.at[layer + 1], chunk, scaled(quarters(result[:, :256])))
        if hold:
            pl.when(jnp.logical_not(holds))(exchange(layer + 1, chunk, partner).start)
        else:
            exchange(layer + 1, chunk, partner).start()
        kept[layer + 1, chunk] = result[:, 256:].astype(jnp.bfloat16)

    advance(0, 0, core, arrived=True)

    @pl.loop(1, EARLY + 1)
    def _(chunk):
        advance(0, chunk, core)
        advance(1, chunk - 1, partner_g)

    @pl.loop(EARLY + 1, CHUNKS)
    def _(chunk):
        advance(0, chunk, core)
        advance(1, chunk - 1, partner_f, hold=True)

    advance(1, CHUNKS - 1, partner_f, hold=True)

    def relay(chunk, partner):
        exchange(2, chunk, core).wait_recv()
        exchange(3, chunk, partner).start()

    @pl.when(holds)
    def _():
        relay(EARLY, partner_g)

        @pl.loop(EARLY, CHUNKS)
        def _(chunk):
            exchange(2, chunk, partner_f).start()

    @pl.loop(0, EARLY)
    def _(chunk):
        relay(chunk, partner_f)

    @pl.loop(EARLY + held, CHUNKS)
    def _(chunk):
        relay(chunk, partner_g)

    @pl.loop(0, CHUNKS)
    def _(chunk):
        exchange(3, chunk, core).wait_recv()
        result = gate(2, 3, chunk)
        for half in range(2):
            start = half * 2 * ROWS + chunk * 2 * STEP
            for part, value in enumerate(quarters(result[:, half * 256 : half * 256 + 256])):
                out_v[pl.ds(start + part, PAIRS, stride=4), :] = value
            store(half, chunk).start()

    @pl.loop(0, CHUNKS)
    def _(chunk):
        for stage in range(4):
            exchange(stage, chunk, core).wait_send()
        for half in range(2):
            store(half, chunk).wait()


def on_device(amplitudes, gates, qubit_sets):
    rows = amplitudes.reshape(2, 2 * ROWS, 128).transpose(1, 0, 2).reshape(4 * ROWS, 128)
    out = pl.pallas_call(
        kernel,
        out_shape=jax.ShapeDtypeStruct((4 * ROWS, 128), jnp.float32),
        in_specs=[
            pl.BlockSpec(memory_space=pl.ANY),
            pl.BlockSpec(memory_space=pl.ANY),
            pl.BlockSpec(memory_space=pl.ANY),
        ],
        out_specs=pl.BlockSpec(memory_space=pl.ANY),
        scratch_shapes=[
            pltpu.SMEM((LAYERS, 7), jnp.int32),
            pltpu.VMEM((LAYERS, 2, 128, 128), jnp.float32),
            pltpu.VMEM((4 * ROWS, 128), jnp.float32),
            pltpu.VMEM((4 * ROWS, 128), jnp.float32),
            pltpu.VMEM((LAYERS, 512, 512), jnp.bfloat16),
            pltpu.VMEM((3, CHUNKS, STEP, 256), jnp.bfloat16),
            pltpu.VMEM((4, CHUNKS, STEP, 256), jnp.bfloat16),
            pltpu.VMEM((3, CHUNKS, STEP, 256), jnp.bfloat16),
            pltpu.SemaphoreType.DMA((CHUNKS,)),
            pltpu.SemaphoreType.DMA((3,)),
            pltpu.SemaphoreType.DMA((4, CHUNKS)),
            pltpu.SemaphoreType.DMA((4, CHUNKS)),
            pltpu.SemaphoreType.DMA((2, CHUNKS)),
        ],
        compiler_params=pltpu.CompilerParams(
            collective_id=0, has_side_effects=True, vmem_limit_bytes=60 * 1024 * 1024
        ),
        name="layers",
    )(qubit_sets, gates, rows)
    return out.reshape(2 * ROWS, 2, 128).transpose(1, 0, 2).reshape(2, 2 * ROWS * 128)


def solution(mesh):
    in_specs = (P(None, ("wide", "mid", "narrow")), P(), P())
    out_specs = P(None, ("wide", "mid", "narrow"))
    return jax.shard_map(
        on_device, mesh=mesh, in_specs=in_specs, out_specs=out_specs, check_vma=False
    )
```

```python
import functools

import jax
import jax.numpy as jnp
from jax import lax
from jax.experimental import pallas as pl
from jax.experimental.pallas import tpu as pltpu
from jax.sharding import PartitionSpec as P

LAYERS = 3
ROWS = 1024
CHUNKS = 8
STEP = ROWS // CHUNKS
PAIRS = STEP // 2
EARLY = CHUNKS // 2


def scaled(parts):
    peak = jnp.maximum(
        jnp.maximum(jnp.abs(parts[0]), jnp.abs(parts[1])),
        jnp.maximum(jnp.abs(parts[2]), jnp.abs(parts[3])),
    )
    magnitude = jnp.max(peak, axis=1, keepdims=True) + 1e-06
    scale = magnitude.astype(jnp.bfloat16).astype(jnp.float32)
    inverse = 1.0 / scale
    coded = [(part * inverse).astype(jnp.bfloat16).astype(jnp.float32) for part in parts]
    return [(part * scale).astype(jnp.bfloat16) for part in coded]


def put(ref, chunk, parts):
    ref[chunk, :PAIRS, :128] = parts[0]
    ref[chunk, :PAIRS, 128:] = parts[1]
    ref[chunk, PAIRS:, :128] = parts[2]
    ref[chunk, PAIRS:, 128:] = parts[3]


def quarters(tile):
    return [tile[:PAIRS, :128], tile[:PAIRS, 128:], tile[PAIRS:, :128], tile[PAIRS:, 128:]]


def spread_gate(layer, own, following, gates_ref, sets_ref, weights):
    cells = lax.broadcasted_iota(jnp.int32, (256, 128), 0)
    wanted = lax.broadcasted_iota(jnp.int32, (256, 128), 1)
    cell_in = lax.broadcasted_iota(jnp.int32, (256, 256), 0)
    cell_out = lax.broadcasted_iota(jnp.int32, (256, 256), 1)
    gate_index = jnp.zeros((256, 128), jnp.int32)
    spare = jnp.int32(28)
    for bit_pos in range(7):
        qubit = sets_ref[layer, bit_pos]
        place = jnp.where(qubit == 17, 7, qubit)
        spare = spare - place
        gate_index = gate_index + (((cells >> place) & 1) << bit_pos)
    select = (gate_index == wanted).astype(jnp.float32).astype(jnp.bfloat16)
    same = ((cell_in >> spare) & 1) == ((cell_out >> spare) & 1)
    last_dims = (((1,), (1,)), ((), ()))
    spreads = []
    for part in range(2):
        matrix = gates_ref[layer, part].astype(jnp.bfloat16)
        half_way = lax.dot_general(select, matrix, last_dims, preferred_element_type=jnp.float32)
        whole = lax.dot_general(
            half_way.astype(jnp.bfloat16), select, last_dims, preferred_element_type=jnp.float32
        )
        spreads.append(jnp.where(same, whole, 0.0))
    real, imag = spreads
    for u_in in range(2):
        row = pl.multiple_of(lax.rem(u_in + own + 1, 2) * 256, 256)
        for u_out in range(2):
            if following is None:
                column = u_out * 256
            else:
                column = pl.multiple_of(lax.rem(u_out + following + 1, 2) * 256, 256)
            re = real[u_in * 128 : u_in * 128 + 128, u_out * 128 : u_out * 128 + 128].astype(jnp.bfloat16)
            im = imag[u_in * 128 : u_in * 128 + 128, u_out * 128 : u_out * 128 + 128].astype(jnp.bfloat16)
            weights[layer, pl.ds(row, 128), pl.ds(column, 128)] = re
            weights[layer, pl.ds(row, 128), pl.ds(column + 128, 128)] = im
            weights[layer, pl.ds(row + 128, 128), pl.ds(column, 128)] = -im
            weights[layer, pl.ds(row + 128, 128), pl.ds(column + 128, 128)] = re


def kernel(
    sets_hbm,
    gates_hbm,
    x_ref,
    out_ref,
    sets_ref,
    gates_ref,
    x_v,
    weights,
    send,
    recv,
    kept,
    load_sem,
    rest_sem,
    send_sem,
    recv_sem,
    ready_sem,
):
    wide = lax.axis_index("wide")
    narrow = lax.axis_index("narrow")
    n_wide = lax.axis_size("wide")
    own = [wide // (n_wide // 2), lax.rem(wide, 2), narrow]
    across = lax.rem(wide + n_wide // 2, n_wide)
    partner_f = {"wide": across}
    partner_g = {"wide": across, "narrow": 1 - narrow}
    core = {"wide": wide + 1 - 2 * own[1]}

    barrier = pltpu.get_barrier_semaphore()
    lower = narrow == 0

    def greet(semaphore, partner):
        pl.semaphore_signal(semaphore, inc=1, device_id=partner, device_id_type=pl.DeviceIdType.MESH)

    greet(barrier, partner_f)
    greet(barrier, core)

    @pl.when(lower)
    def _():
        greet(barrier, partner_g)


    away = pl.multiple_of((1 - own[0]) * 2 * ROWS, 2 * ROWS)
    home = pl.multiple_of(own[0] * 2 * ROWS, 2 * ROWS)

    def load(chunk):
        rows = pl.ds(away + chunk * 2 * STEP, 2 * STEP)
        return pltpu.make_async_copy(x_ref.at[rows], x_v.at[rows], load_sem.at[chunk])

    rest = [
        pltpu.make_async_copy(x_ref.at[pl.ds(home, 2 * ROWS)], x_v.at[pl.ds(home, 2 * ROWS)], rest_sem.at[0]),
        pltpu.make_async_copy(gates_hbm, gates_ref, rest_sem.at[1]),
        pltpu.make_async_copy(sets_hbm, sets_ref, rest_sem.at[2]),
    ]

    def exchange(stage, chunk, partner):
        source = send.at[stage, chunk] if stage < 3 else recv.at[2, chunk]
        return pltpu.make_async_remote_copy(
            src_ref=source,
            dst_ref=recv.at[stage, chunk],
            send_sem=send_sem.at[stage, chunk],
            recv_sem=recv_sem.at[stage, chunk],
            device_id=partner,
            device_id_type=pl.DeviceIdType.MESH,
        )

    def read(base, chunk):
        start = base + chunk * 2 * STEP
        return [x_v[pl.ds(start + part, PAIRS, stride=4), :] for part in range(4)]

    for chunk in range(CHUNKS):
        load(chunk).start()
    for copy in rest:
        copy.start()

    def first(chunk):
        load(chunk).wait()
        put(send.at[0], chunk, scaled(read(away, chunk)))

    def send_first():
        exchange(0, 0, partner_f).start()

        @pl.loop(1, CHUNKS)
        def _(chunk):
            first(chunk)
            exchange(0, chunk, partner_f).start()

    def prepare():
        for copy in rest:
            copy.wait()
        spread_gate(0, own[0], own[1], gates_ref, sets_ref, weights)

        @pl.loop(0, CHUNKS)
        def _(chunk):
            put(kept.at[0], chunk, [part.astype(jnp.bfloat16) for part in read(home, chunk)])

        spread_gate(1, own[1], own[2], gates_ref, sets_ref, weights)
        spread_gate(2, own[2], None, gates_ref, sets_ref, weights)
        exchange(0, 0, core).wait_recv()

    first(0)
    @pl.when(lower)
    def _():
        pl.semaphore_wait(barrier, 2)

    @pl.when(jnp.logical_not(lower))
    def _():
        pl.semaphore_wait(barrier, 3)
        greet(ready_sem, partner_g)

    send_first()
    prepare()

    @pl.when(lower)
    def _():
        pl.semaphore_wait(ready_sem, 1)

    holds = lax.rem(wide // (n_wide // 8), 8) == 7
    held = jnp.where(holds, 1, 0)

    def gate(layer, stage, chunk):
        block = jnp.concatenate([recv[stage, chunk], kept[layer, chunk]], axis=1)
        return jnp.dot(block, weights[layer], preferred_element_type=jnp.float32)

    def advance(layer, chunk, partner, arrived=False, hold=False):
        if not arrived:
            exchange(layer, chunk, core).wait_recv()
        result = gate(layer, layer, chunk)
        put(send.at[layer + 1], chunk, scaled(quarters(result[:, :256])))
        if hold:
            pl.when(jnp.logical_or(jnp.logical_not(holds), chunk < EARLY + 1))(exchange(layer + 1, chunk, partner).start)
        else:
            exchange(layer + 1, chunk, partner).start()
        kept[layer + 1, chunk] = result[:, 256:].astype(jnp.bfloat16)

    advance(0, 0, core, arrived=True)

    @pl.loop(1, EARLY + 1)
    def _(chunk):
        advance(0, chunk, core)
        advance(1, chunk - 1, partner_g)

    @pl.loop(EARLY + 1, CHUNKS)
    def _(chunk):
        advance(0, chunk, core)
        advance(1, chunk - 1, partner_f, hold=True)

    advance(1, CHUNKS - 1, partner_f, hold=True)

    def relay(chunk, partner):
        exchange(2, chunk, core).wait_recv()
        exchange(3, chunk, partner).start()

    @pl.when(holds)
    def _():
        relay(EARLY, partner_g)

        @pl.loop(EARLY + 1, CHUNKS)
        def _(chunk):
            exchange(2, chunk, partner_f).start()

    @pl.loop(0, EARLY)
    def _(chunk):
        relay(chunk, partner_f)

    @pl.loop(EARLY + held, CHUNKS)
    def _(chunk):
        relay(chunk, partner_g)

    @pl.loop(0, CHUNKS)
    def _(chunk):
        exchange(3, chunk, core).wait_recv()
        result = gate(2, 3, chunk)
        for half in range(2):
            start = half * 2 * ROWS + chunk * 2 * STEP
            for part, value in enumerate(quarters(result[:, half * 256 : half * 256 + 256])):
                out_ref[pl.ds(start + part, PAIRS, stride=4), :] = value

    @pl.loop(0, CHUNKS)
    def _(chunk):
        for stage in range(4):
            exchange(stage, chunk, core).wait_send()


def on_device(amplitudes, gates, qubit_sets):
    rows = amplitudes.reshape(2, 2 * ROWS, 128).transpose(1, 0, 2).reshape(4 * ROWS, 128)
    out = pl.pallas_call(
        kernel,
        out_shape=pltpu.VMEM((4 * ROWS, 128), jnp.float32),
        in_specs=[
            pl.BlockSpec(memory_space=pl.ANY),
            pl.BlockSpec(memory_space=pl.ANY),
            pl.BlockSpec(memory_space=pl.ANY),
        ],
        out_specs=pl.BlockSpec(memory_space=pltpu.VMEM),
        scratch_shapes=[
            pltpu.SMEM((LAYERS, 7), jnp.int32),
            pltpu.VMEM((LAYERS, 2, 128, 128), jnp.float32),
            pltpu.VMEM((4 * ROWS, 128), jnp.float32),
            pltpu.VMEM((LAYERS, 512, 512), jnp.bfloat16),
            pltpu.VMEM((3, CHUNKS, STEP, 256), jnp.bfloat16),
            pltpu.VMEM((4, CHUNKS, STEP, 256), jnp.bfloat16),
            pltpu.VMEM((3, CHUNKS, STEP, 256), jnp.bfloat16),
            pltpu.SemaphoreType.DMA((CHUNKS,)),
            pltpu.SemaphoreType.DMA((3,)),
            pltpu.SemaphoreType.DMA((4, CHUNKS)),
            pltpu.SemaphoreType.DMA((4, CHUNKS)),
            pltpu.SemaphoreType.REGULAR,
        ],
        compiler_params=pltpu.CompilerParams(
            collective_id=0, has_side_effects=True, vmem_limit_bytes=60 * 1024 * 1024
        ),
        name="layers",
    )(qubit_sets, gates, rows)
    return out.reshape(2 * ROWS, 2, 128).transpose(1, 0, 2).reshape(2, 2 * ROWS * 128)


def solution(mesh):
    in_specs = (P(None, ("wide", "mid", "narrow")), P(), P())
    out_specs = P(None, ("wide", "mid", "narrow"))
    return jax.shard_map(
        on_device, mesh=mesh, in_specs=in_specs, out_specs=out_specs, check_vma=False
    )
```

```python
import functools

import jax
import jax.numpy as jnp
from jax import lax
from jax.experimental import pallas as pl
from jax.experimental.pallas import tpu as pltpu
from jax.sharding import PartitionSpec as P

LAYERS = 3
ROWS = 1024
CHUNKS = 8
STEP = ROWS // CHUNKS
PAIRS = STEP // 2
EARLY = CHUNKS // 2


def scaled(parts):
    peak = jnp.maximum(
        jnp.maximum(jnp.abs(parts[0]), jnp.abs(parts[1])),
        jnp.maximum(jnp.abs(parts[2]), jnp.abs(parts[3])),
    )
    magnitude = jnp.max(peak, axis=1, keepdims=True) + 1e-06
    scale = magnitude.astype(jnp.bfloat16).astype(jnp.float32)
    inverse = 1.0 / scale
    coded = [(part * inverse).astype(jnp.bfloat16).astype(jnp.float32) for part in parts]
    return [(part * scale).astype(jnp.bfloat16) for part in coded]


def put(ref, chunk, parts):
    ref[chunk, :PAIRS, :128] = parts[0]
    ref[chunk, :PAIRS, 128:] = parts[1]
    ref[chunk, PAIRS:, :128] = parts[2]
    ref[chunk, PAIRS:, 128:] = parts[3]


def quarters(tile):
    return [tile[:PAIRS, :128], tile[:PAIRS, 128:], tile[PAIRS:, :128], tile[PAIRS:, 128:]]


def spread_gate(layer, own, following, gates_ref, sets_ref, weights):
    cells = lax.broadcasted_iota(jnp.int32, (256, 128), 0)
    wanted = lax.broadcasted_iota(jnp.int32, (256, 128), 1)
    cell_in = lax.broadcasted_iota(jnp.int32, (256, 256), 0)
    cell_out = lax.broadcasted_iota(jnp.int32, (256, 256), 1)
    gate_index = jnp.zeros((256, 128), jnp.int32)
    spare = jnp.int32(28)
    for bit_pos in range(7):
        qubit = sets_ref[layer, bit_pos]
        place = jnp.where(qubit == 17, 7, qubit)
        spare = spare - place
        gate_index = gate_index + (((cells >> place) & 1) << bit_pos)
    select = (gate_index == wanted).astype(jnp.float32).astype(jnp.bfloat16)
    same = ((cell_in >> spare) & 1) == ((cell_out >> spare) & 1)
    last_dims = (((1,), (1,)), ((), ()))
    spreads = []
    for part in range(2):
        matrix = gates_ref[layer, part].astype(jnp.bfloat16)
        half_way = lax.dot_general(select, matrix, last_dims, preferred_element_type=jnp.float32)
        whole = lax.dot_general(
            half_way.astype(jnp.bfloat16), select, last_dims, preferred_element_type=jnp.float32
        )
        spreads.append(jnp.where(same, whole, 0.0))
    real, imag = spreads
    for u_in in range(2):
        row = pl.multiple_of(lax.rem(u_in + own + 1, 2) * 256, 256)
        for u_out in range(2):
            if following is None:
                column = u_out * 256
            else:
                column = pl.multiple_of(lax.rem(u_out + following + 1, 2) * 256, 256)
            re = real[u_in * 128 : u_in * 128 + 128, u_out * 128 : u_out * 128 + 128].astype(jnp.bfloat16)
            im = imag[u_in * 128 : u_in * 128 + 128, u_out * 128 : u_out * 128 + 128].astype(jnp.bfloat16)
            weights[layer, pl.ds(row, 128), pl.ds(column, 128)] = re
            weights[layer, pl.ds(row, 128), pl.ds(column + 128, 128)] = im
            weights[layer, pl.ds(row + 128, 128), pl.ds(column, 128)] = -im
            weights[layer, pl.ds(row + 128, 128), pl.ds(column + 128, 128)] = re


def kernel(
    sets_hbm,
    gates_hbm,
    x_ref,
    out_ref,
    sets_ref,
    gates_ref,
    x_v,
    weights,
    send,
    recv,
    kept,
    load_sem,
    rest_sem,
    send_sem,
    recv_sem,
    ready_sem,
):
    wide = lax.axis_index("wide")
    narrow = lax.axis_index("narrow")
    n_wide = lax.axis_size("wide")
    own = [wide // (n_wide // 2), lax.rem(wide, 2), narrow]
    across = lax.rem(wide + n_wide // 2, n_wide)
    partner_f = {"wide": across}
    partner_g = {"wide": across, "narrow": 1 - narrow}
    core = {"wide": wide + 1 - 2 * own[1]}

    barrier = pltpu.get_barrier_semaphore()
    lower = narrow == 0

    def greet(semaphore, partner):
        pl.semaphore_signal(semaphore, inc=1, device_id=partner, device_id_type=pl.DeviceIdType.MESH)

    greet(barrier, partner_f)
    greet(barrier, core)

    @pl.when(lower)
    def _():
        greet(barrier, partner_g)

    away = pl.multiple_of((1 - own[0]) * 2 * ROWS, 2 * ROWS)
    home = pl.multiple_of(own[0] * 2 * ROWS, 2 * ROWS)

    def load(chunk):
        rows = pl.ds(away + chunk * 2 * STEP, 2 * STEP)
        return pltpu.make_async_copy(x_ref.at[rows], x_v.at[rows], load_sem.at[chunk])

    rest = [
        pltpu.make_async_copy(x_ref.at[pl.ds(home, 2 * ROWS)], x_v.at[pl.ds(home, 2 * ROWS)], rest_sem.at[0]),
        pltpu.make_async_copy(gates_hbm, gates_ref, rest_sem.at[1]),
        pltpu.make_async_copy(sets_hbm, sets_ref, rest_sem.at[2]),
    ]

    def exchange(stage, chunk, partner):
        source = [send.at[0], send.at[1], send.at[2], recv.at[2], send.at[2], recv.at[4]][stage]
        target = [0, 1, 2, 3, 4, 3][stage]
        return pltpu.make_async_remote_copy(
            src_ref=source.at[chunk],
            dst_ref=recv.at[target, chunk],
            send_sem=send_sem.at[[0, 1, 2, 3, 2, 4][stage], chunk],
            recv_sem=recv_sem.at[target, chunk],
            device_id=partner,
            device_id_type=pl.DeviceIdType.MESH,
        )

    def read(base, chunk):
        start = base + chunk * 2 * STEP
        return [x_v[pl.ds(start + part, PAIRS, stride=4), :] for part in range(4)]

    load(0).start()

    def first(chunk):
        load(chunk).wait()
        put(send.at[0], chunk, scaled(read(away, chunk)))

    def send_first():
        exchange(0, 0, partner_f).start()

        @pl.loop(1, CHUNKS)
        def _(chunk):
            first(chunk)
            exchange(0, chunk, partner_f).start()

    def prepare():
        for copy in rest:
            copy.wait()
        spread_gate(0, own[0], own[1], gates_ref, sets_ref, weights)

        @pl.loop(0, CHUNKS)
        def _(chunk):
            put(kept.at[0], chunk, [part.astype(jnp.bfloat16) for part in read(home, chunk)])

        spread_gate(1, own[1], own[2], gates_ref, sets_ref, weights)
        spread_gate(2, own[2], None, gates_ref, sets_ref, weights)
        exchange(0, 0, core).wait_recv()

    first(0)

    for chunk in range(1, CHUNKS):
        load(chunk).start()
    for copy in rest:
        copy.start()

    @pl.when(lower)
    def _():
        pl.semaphore_wait(barrier, 2)

    @pl.when(jnp.logical_not(lower))
    def _():
        pl.semaphore_wait(barrier, 3)
        greet(ready_sem, partner_g)

    send_first()
    prepare()

    @pl.when(lower)
    def _():
        pl.semaphore_wait(ready_sem, 1)

    z_low = wide // (n_wide // 8)
    holds = z_low == 7
    held = jnp.where(holds, 1, 0)
    early_lower = EARLY + jnp.where(lax.rem(z_low, 4) == 3, 1, 0)
    early = jnp.where(lower, early_lower, EARLY)
    early_from_g = jnp.where(lower, EARLY, early_lower)

    def gate(layer, stage, chunk):
        block = jnp.concatenate([recv[stage, chunk], kept[layer, chunk]], axis=1)
        return jnp.dot(block, weights[layer], preferred_element_type=jnp.float32)

    def advance(layer, chunk, stage, partner, arrived=False):
        if not arrived:
            exchange(layer, chunk, core).wait_recv()
        result = gate(layer, layer, chunk)
        put(send.at[layer + 1], chunk, scaled(quarters(result[:, :256])))
        if stage == 4:
            pl.when(jnp.logical_not(holds))(exchange(4, chunk, partner_f).start)
        else:
            exchange(stage, chunk, partner).start()
        kept[layer + 1, chunk] = result[:, 256:].astype(jnp.bfloat16)

    advance(0, 0, 1, core, arrived=True)

    @pl.loop(1, early + 1)
    def _(chunk):
        advance(0, chunk, 1, core)
        advance(1, chunk - 1, 2, partner_g)

    @pl.loop(early + 1, CHUNKS)
    def _(chunk):
        advance(0, chunk, 1, core)
        advance(1, chunk - 1, 4, partner_f)

    advance(1, CHUNKS - 1, 4, partner_f)

    def relay_to_g(chunk):
        exchange(4, chunk, core).wait_recv()
        exchange(5, chunk, partner_g).start()

    @pl.when(holds)
    def _():
        relay_to_g(early)

        @pl.loop(early, CHUNKS)
        def _(chunk):
            exchange(4, chunk, partner_f).start()

    @pl.loop(0, early_from_g)
    def _(chunk):
        exchange(2, chunk, core).wait_recv()
        exchange(3, chunk, partner_f).start()

    @pl.loop(early + held, CHUNKS)
    def _(chunk):
        relay_to_g(chunk)

    turn_from = jnp.where(z_low == 0, 0, early_from_g)

    @pl.loop(0, CHUNKS)
    def _(turn):
        chunk = lax.rem(turn + turn_from, CHUNKS)
        exchange(3, chunk, core).wait_recv()
        result = gate(2, 3, chunk)
        for half in range(2):
            start = half * 2 * ROWS + chunk * 2 * STEP
            for part, value in enumerate(quarters(result[:, half * 256 : half * 256 + 256])):
                out_ref[pl.ds(start + part, PAIRS, stride=4), :] = value

    @pl.loop(0, CHUNKS)
    def _(chunk):
        for stage in range(3):
            exchange(stage, chunk, core).wait_send()

    @pl.loop(0, early_from_g)
    def _(chunk):
        exchange(3, chunk, core).wait_send()

    @pl.loop(early, CHUNKS)
    def _(chunk):
        exchange(5, chunk, core).wait_send()


def on_device(amplitudes, gates, qubit_sets):
    rows = amplitudes.reshape(2, 2 * ROWS, 128).transpose(1, 0, 2).reshape(4 * ROWS, 128)
    out = pl.pallas_call(
        kernel,
        out_shape=pltpu.VMEM((4 * ROWS, 128), jnp.float32),
        in_specs=[
            pl.BlockSpec(memory_space=pl.ANY),
            pl.BlockSpec(memory_space=pl.ANY),
            pl.BlockSpec(memory_space=pl.ANY),
        ],
        out_specs=pl.BlockSpec(memory_space=pltpu.VMEM),
        scratch_shapes=[
            pltpu.SMEM((LAYERS, 7), jnp.int32),
            pltpu.VMEM((LAYERS, 2, 128, 128), jnp.float32),
            pltpu.VMEM((4 * ROWS, 128), jnp.float32),
            pltpu.VMEM((LAYERS, 512, 512), jnp.bfloat16),
            pltpu.VMEM((3, CHUNKS, STEP, 256), jnp.bfloat16),
            pltpu.VMEM((5, CHUNKS, STEP, 256), jnp.bfloat16),
            pltpu.VMEM((3, CHUNKS, STEP, 256), jnp.bfloat16),
            pltpu.SemaphoreType.DMA((CHUNKS,)),
            pltpu.SemaphoreType.DMA((3,)),
            pltpu.SemaphoreType.DMA((5, CHUNKS)),
            pltpu.SemaphoreType.DMA((5, CHUNKS)),
            pltpu.SemaphoreType.REGULAR,
        ],
        compiler_params=pltpu.CompilerParams(
            collective_id=0, has_side_effects=True, vmem_limit_bytes=60 * 1024 * 1024
        ),
        name="layers",
    )(qubit_sets, gates, rows)
    return out.reshape(2 * ROWS, 2, 128).transpose(1, 0, 2).reshape(2, 2 * ROWS * 128)


def solution(mesh):
    in_specs = (P(None, ("wide", "mid", "narrow")), P(), P())
    out_specs = P(None, ("wide", "mid", "narrow"))
    return jax.shard_map(
        on_device, mesh=mesh, in_specs=in_specs, out_specs=out_specs, check_vma=False
    )
```

```python
import functools

import jax
import jax.numpy as jnp
from jax import lax
from jax.experimental import pallas as pl
from jax.experimental.pallas import tpu as pltpu
from jax.sharding import PartitionSpec as P

LAYERS = 3
ROWS = 1024
CHUNKS = 8
STEP = ROWS // CHUNKS
PAIRS = STEP // 2
EARLY = CHUNKS // 2


def scaled(parts):
    peak = jnp.maximum(
        jnp.maximum(jnp.abs(parts[0]), jnp.abs(parts[1])),
        jnp.maximum(jnp.abs(parts[2]), jnp.abs(parts[3])),
    )
    magnitude = jnp.max(peak, axis=1, keepdims=True) + 1e-06
    scale = magnitude.astype(jnp.bfloat16).astype(jnp.float32)
    inverse = 1.0 / scale
    coded = [(part * inverse).astype(jnp.bfloat16).astype(jnp.float32) for part in parts]
    return [(part * scale).astype(jnp.bfloat16) for part in coded]


def put(ref, chunk, parts):
    ref[chunk, :PAIRS, :128] = parts[0]
    ref[chunk, :PAIRS, 128:] = parts[1]
    ref[chunk, PAIRS:, :128] = parts[2]
    ref[chunk, PAIRS:, 128:] = parts[3]


def quarters(tile):
    return [tile[:PAIRS, :128], tile[:PAIRS, 128:], tile[PAIRS:, :128], tile[PAIRS:, 128:]]


def spread_gate(layer, own, following, gates_ref, sets_ref, weights):
    cells = lax.broadcasted_iota(jnp.int32, (256, 128), 0)
    wanted = lax.broadcasted_iota(jnp.int32, (256, 128), 1)
    cell_in = lax.broadcasted_iota(jnp.int32, (256, 256), 0)
    cell_out = lax.broadcasted_iota(jnp.int32, (256, 256), 1)
    gate_index = jnp.zeros((256, 128), jnp.int32)
    spare = jnp.int32(28)
    for bit_pos in range(7):
        qubit = sets_ref[layer, bit_pos]
        place = jnp.where(qubit == 17, 7, qubit)
        spare = spare - place
        gate_index = gate_index + (((cells >> place) & 1) << bit_pos)
    select = (gate_index == wanted).astype(jnp.float32).astype(jnp.bfloat16)
    same = ((cell_in >> spare) & 1) == ((cell_out >> spare) & 1)
    last_dims = (((1,), (1,)), ((), ()))
    spreads = []
    for part in range(2):
        matrix = gates_ref[layer, part].astype(jnp.bfloat16)
        half_way = lax.dot_general(select, matrix, last_dims, preferred_element_type=jnp.float32)
        whole = lax.dot_general(
            half_way.astype(jnp.bfloat16), select, last_dims, preferred_element_type=jnp.float32
        )
        spreads.append(jnp.where(same, whole, 0.0))
    real, imag = spreads
    for u_in in range(2):
        row = pl.multiple_of(lax.rem(u_in + own + 1, 2) * 256, 256)
        for u_out in range(2):
            if following is None:
                column = u_out * 256
            else:
                column = pl.multiple_of(lax.rem(u_out + following + 1, 2) * 256, 256)
            re = real[u_in * 128 : u_in * 128 + 128, u_out * 128 : u_out * 128 + 128].astype(jnp.bfloat16)
            im = imag[u_in * 128 : u_in * 128 + 128, u_out * 128 : u_out * 128 + 128].astype(jnp.bfloat16)
            weights[layer, pl.ds(row, 128), pl.ds(column, 128)] = re
            weights[layer, pl.ds(row, 128), pl.ds(column + 128, 128)] = im
            weights[layer, pl.ds(row + 128, 128), pl.ds(column, 128)] = -im
            weights[layer, pl.ds(row + 128, 128), pl.ds(column + 128, 128)] = re


def kernel(
    sets_hbm,
    gates_hbm,
    x_ref,
    out_ref,
    sets_ref,
    gates_ref,
    x_v,
    weights,
    send,
    recv,
    kept,
    load_sem,
    rest_sem,
    send_sem,
    recv_sem,
    ready_sem,
):
    wide = lax.axis_index("wide")
    narrow = lax.axis_index("narrow")
    n_wide = lax.axis_size("wide")
    own = [wide // (n_wide // 2), lax.rem(wide, 2), narrow]
    across = lax.rem(wide + n_wide // 2, n_wide)
    partner_f = {"wide": across}
    partner_g = {"wide": across, "narrow": 1 - narrow}
    core = {"wide": wide + 1 - 2 * own[1]}

    barrier = pltpu.get_barrier_semaphore()
    lower = narrow == 0

    def greet(semaphore, partner):
        pl.semaphore_signal(semaphore, inc=1, device_id=partner, device_id_type=pl.DeviceIdType.MESH)

    greet(barrier, partner_f)
    greet(barrier, core)

    @pl.when(lower)
    def _():
        greet(barrier, partner_g)

    away = pl.multiple_of((1 - own[0]) * 2 * ROWS, 2 * ROWS)
    home = pl.multiple_of(own[0] * 2 * ROWS, 2 * ROWS)

    def load(chunk):
        rows = pl.ds(away + chunk * 2 * STEP, 2 * STEP)
        return pltpu.make_async_copy(x_ref.at[rows], x_v.at[rows], load_sem.at[chunk])

    rest = [
        pltpu.make_async_copy(x_ref.at[pl.ds(home, 2 * ROWS)], x_v.at[pl.ds(home, 2 * ROWS)], rest_sem.at[0]),
        pltpu.make_async_copy(gates_hbm, gates_ref, rest_sem.at[1]),
        pltpu.make_async_copy(sets_hbm, sets_ref, rest_sem.at[2]),
    ]

    def exchange(stage, chunk, partner):
        source = [send.at[0], send.at[1], send.at[2], recv.at[2], send.at[2], recv.at[4]][stage]
        target = [0, 1, 2, 3, 4, 3][stage]
        return pltpu.make_async_remote_copy(
            src_ref=source.at[chunk],
            dst_ref=recv.at[target, chunk],
            send_sem=send_sem.at[[0, 1, 2, 3, 2, 4][stage], chunk],
            recv_sem=recv_sem.at[target, chunk],
            device_id=partner,
            device_id_type=pl.DeviceIdType.MESH,
        )

    def read(base, chunk):
        start = base + chunk * 2 * STEP
        return [x_v[pl.ds(start + part, PAIRS, stride=4), :] for part in range(4)]

    load(0).start()

    def first(chunk):
        load(chunk).wait()
        put(send.at[0], chunk, scaled(read(away, chunk)))

    def send_first():
        exchange(0, 0, partner_f).start()

        @pl.loop(1, CHUNKS)
        def _(chunk):
            first(chunk)
            exchange(0, chunk, partner_f).start()

    def prepare():
        for copy in rest:
            copy.wait()
        spread_gate(0, own[0], own[1], gates_ref, sets_ref, weights)

        @pl.loop(0, CHUNKS)
        def _(chunk):
            put(kept.at[0], chunk, [part.astype(jnp.bfloat16) for part in read(home, chunk)])

        spread_gate(1, own[1], own[2], gates_ref, sets_ref, weights)
        spread_gate(2, own[2], None, gates_ref, sets_ref, weights)
        exchange(0, 0, core).wait_recv()

    first(0)

    for chunk in range(1, CHUNKS):
        load(chunk).start()
    for copy in rest:
        copy.start()

    @pl.when(lower)
    def _():
        pl.semaphore_wait(barrier, 2)

    @pl.when(jnp.logical_not(lower))
    def _():
        pl.semaphore_wait(barrier, 3)
        greet(ready_sem, partner_g)

    send_first()
    prepare()

    @pl.when(lower)
    def _():
        pl.semaphore_wait(ready_sem, 1)

    z_low = wide // (n_wide // 8)
    holds = z_low == 7
    held = jnp.where(holds, 1, 0)
    early_lower = EARLY + jnp.where(lax.rem(z_low, 4) == 3, 1, 0)
    early = jnp.where(lower, early_lower, EARLY)
    early_from_g = jnp.where(lower, EARLY, early_lower)

    def gate(layer, stage, chunk):
        block = jnp.concatenate([recv[stage, chunk], kept[layer, chunk]], axis=1)
        return jnp.dot(block, weights[layer], preferred_element_type=jnp.float32)

    def advance(layer, chunk, stage, partner, arrived=False):
        if not arrived:
            exchange(layer, chunk, core).wait_recv()
        result = gate(layer, layer, chunk)
        put(send.at[layer + 1], chunk, scaled(quarters(result[:, :256])))
        if stage == 4:
            pl.when(jnp.logical_not(holds))(exchange(4, chunk, partner_f).start)
        else:
            exchange(stage, chunk, partner).start()
        kept[layer + 1, chunk] = result[:, 256:].astype(jnp.bfloat16)

    advance(0, 0, 1, core, arrived=True)

    @pl.loop(1, early + 1)
    def _(chunk):
        advance(0, chunk, 1, core)
        advance(1, chunk - 1, 2, partner_g)

    @pl.loop(early + 1, CHUNKS)
    def _(chunk):
        advance(0, chunk, 1, core)
        advance(1, chunk - 1, 4, partner_f)

    advance(1, CHUNKS - 1, 4, partner_f)

    def relay_to_g(chunk):
        exchange(4, chunk, core).wait_recv()
        exchange(5, chunk, partner_g).start()

    @pl.when(holds)
    def _():
        relay_to_g(early)

        @pl.loop(early, CHUNKS)
        def _(chunk):
            exchange(4, chunk, partner_f).start()

    @pl.loop(0, early_from_g)
    def _(chunk):
        exchange(2, chunk, core).wait_recv()
        exchange(3, chunk, partner_f).start()

    @pl.loop(early + held, CHUNKS)
    def _(chunk):
        relay_to_g(chunk)

    @pl.loop(0, CHUNKS)
    def _(chunk):
        for stage in range(2):
            exchange(stage, chunk, core).wait_send()

    turn_from = jnp.where(jnp.logical_and(lower, z_low == 0), 0, early_from_g)

    @pl.loop(0, CHUNKS)
    def _(turn):
        chunk = lax.rem(turn + turn_from, CHUNKS)
        exchange(3, chunk, core).wait_recv()
        result = gate(2, 3, chunk)
        for half in range(2):
            start = half * 2 * ROWS + chunk * 2 * STEP
            for part, value in enumerate(quarters(result[:, half * 256 : half * 256 + 256])):
                out_ref[pl.ds(start + part, PAIRS, stride=4), :] = value

    @pl.loop(0, CHUNKS)
    def _(chunk):
        exchange(2, chunk, core).wait_send()

    @pl.loop(0, early_from_g)
    def _(chunk):
        exchange(3, chunk, core).wait_send()

    @pl.loop(early, CHUNKS)
    def _(chunk):
        exchange(5, chunk, core).wait_send()


def on_device(amplitudes, gates, qubit_sets):
    rows = amplitudes.reshape(2, 2 * ROWS, 128).transpose(1, 0, 2).reshape(4 * ROWS, 128)
    out = pl.pallas_call(
        kernel,
        out_shape=pltpu.VMEM((4 * ROWS, 128), jnp.float32),
        in_specs=[
            pl.BlockSpec(memory_space=pl.ANY),
            pl.BlockSpec(memory_space=pl.ANY),
            pl.BlockSpec(memory_space=pl.ANY),
        ],
        out_specs=pl.BlockSpec(memory_space=pltpu.VMEM),
        scratch_shapes=[
            pltpu.SMEM((LAYERS, 7), jnp.int32),
            pltpu.VMEM((LAYERS, 2, 128, 128), jnp.float32),
            pltpu.VMEM((4 * ROWS, 128), jnp.float32),
            pltpu.VMEM((LAYERS, 512, 512), jnp.bfloat16),
            pltpu.VMEM((3, CHUNKS, STEP, 256), jnp.bfloat16),
            pltpu.VMEM((5, CHUNKS, STEP, 256), jnp.bfloat16),
            pltpu.VMEM((3, CHUNKS, STEP, 256), jnp.bfloat16),
            pltpu.SemaphoreType.DMA((CHUNKS,)),
            pltpu.SemaphoreType.DMA((3,)),
            pltpu.SemaphoreType.DMA((5, CHUNKS)),
            pltpu.SemaphoreType.DMA((5, CHUNKS)),
            pltpu.SemaphoreType.REGULAR,
        ],
        compiler_params=pltpu.CompilerParams(
            collective_id=0, has_side_effects=True, vmem_limit_bytes=60 * 1024 * 1024
        ),
        name="layers",
    )(qubit_sets, gates, rows)
    return out.reshape(2 * ROWS, 2, 128).transpose(1, 0, 2).reshape(2, 2 * ROWS * 128)


def solution(mesh):
    in_specs = (P(None, ("wide", "mid", "narrow")), P(), P())
    out_specs = P(None, ("wide", "mid", "narrow"))
    return jax.shard_map(
        on_device, mesh=mesh, in_specs=in_specs, out_specs=out_specs, check_vma=False
    )
```

```python
import functools

import jax
import jax.numpy as jnp
from jax import lax
from jax.experimental import pallas as pl
from jax.experimental.pallas import tpu as pltpu
from jax.sharding import PartitionSpec as P

LAYERS = 3
ROWS = 1024
CHUNKS = 8
STEP = ROWS // CHUNKS
PAIRS = STEP // 2
EARLY = CHUNKS // 2


def scaled(parts):
    peak = jnp.maximum(
        jnp.maximum(jnp.abs(parts[0]), jnp.abs(parts[1])),
        jnp.maximum(jnp.abs(parts[2]), jnp.abs(parts[3])),
    )
    magnitude = jnp.max(peak, axis=1, keepdims=True) + 1e-06
    scale = magnitude.astype(jnp.bfloat16).astype(jnp.float32)
    inverse = 1.0 / scale
    coded = [(part * inverse).astype(jnp.bfloat16).astype(jnp.float32) for part in parts]
    return [(part * scale).astype(jnp.bfloat16) for part in coded]


def put(ref, chunk, parts):
    ref[chunk, :PAIRS, :128] = parts[0]
    ref[chunk, :PAIRS, 128:] = parts[1]
    ref[chunk, PAIRS:, :128] = parts[2]
    ref[chunk, PAIRS:, 128:] = parts[3]


def quarters(tile):
    return [tile[:PAIRS, :128], tile[:PAIRS, 128:], tile[PAIRS:, :128], tile[PAIRS:, 128:]]


def spread_gate(layer, own, following, gates_ref, sets_ref, weights):
    cells = lax.broadcasted_iota(jnp.int32, (256, 128), 0)
    wanted = lax.broadcasted_iota(jnp.int32, (256, 128), 1)
    cell_in = lax.broadcasted_iota(jnp.int32, (256, 256), 0)
    cell_out = lax.broadcasted_iota(jnp.int32, (256, 256), 1)
    gate_index = jnp.zeros((256, 128), jnp.int32)
    spare = jnp.int32(28)
    for bit_pos in range(7):
        qubit = sets_ref[layer, bit_pos]
        place = jnp.where(qubit == 17, 7, qubit)
        spare = spare - place
        gate_index = gate_index + (((cells >> place) & 1) << bit_pos)
    select = (gate_index == wanted).astype(jnp.float32).astype(jnp.bfloat16)
    same = ((cell_in >> spare) & 1) == ((cell_out >> spare) & 1)
    last_dims = (((1,), (1,)), ((), ()))
    spreads = []
    for part in range(2):
        matrix = gates_ref[layer, part].astype(jnp.bfloat16)
        half_way = lax.dot_general(select, matrix, last_dims, preferred_element_type=jnp.float32)
        whole = lax.dot_general(
            half_way.astype(jnp.bfloat16), select, last_dims, preferred_element_type=jnp.float32
        )
        spreads.append(jnp.where(same, whole, 0.0))
    real, imag = spreads
    for u_in in range(2):
        row = pl.multiple_of(lax.rem(u_in + own + 1, 2) * 256, 256)
        for u_out in range(2):
            if following is None:
                column = u_out * 256
            else:
                column = pl.multiple_of(lax.rem(u_out + following + 1, 2) * 256, 256)
            re = real[u_in * 128 : u_in * 128 + 128, u_out * 128 : u_out * 128 + 128].astype(jnp.bfloat16)
            im = imag[u_in * 128 : u_in * 128 + 128, u_out * 128 : u_out * 128 + 128].astype(jnp.bfloat16)
            weights[layer, pl.ds(row, 128), pl.ds(column, 128)] = re
            weights[layer, pl.ds(row, 128), pl.ds(column + 128, 128)] = im
            weights[layer, pl.ds(row + 128, 128), pl.ds(column, 128)] = -im
            weights[layer, pl.ds(row + 128, 128), pl.ds(column + 128, 128)] = re


def kernel(
    sets_hbm,
    gates_hbm,
    x_ref,
    out_ref,
    sets_ref,
    gates_ref,
    x_v,
    weights,
    send,
    recv,
    kept,
    load_sem,
    rest_sem,
    send_sem,
    recv_sem,
    ready_sem,
):
    wide = lax.axis_index("wide")
    narrow = lax.axis_index("narrow")
    n_wide = lax.axis_size("wide")
    own = [wide // (n_wide // 2), lax.rem(wide, 2), narrow]
    across = lax.rem(wide + n_wide // 2, n_wide)
    partner_f = {"wide": across}
    partner_g = {"wide": across, "narrow": 1 - narrow}
    core = {"wide": wide + 1 - 2 * own[1]}

    barrier = pltpu.get_barrier_semaphore()
    lower = narrow == 0

    def greet(semaphore, partner):
        pl.semaphore_signal(semaphore, inc=1, device_id=partner, device_id_type=pl.DeviceIdType.MESH)

    greet(barrier, partner_f)
    greet(barrier, core)

    @pl.when(lower)
    def _():
        greet(barrier, partner_g)

    away = pl.multiple_of((1 - own[0]) * 2 * ROWS, 2 * ROWS)
    home = pl.multiple_of(own[0] * 2 * ROWS, 2 * ROWS)

    def load(chunk):
        rows = pl.ds(away + chunk * 2 * STEP, 2 * STEP)
        return pltpu.make_async_copy(x_ref.at[rows], x_v.at[rows], load_sem.at[chunk])

    rest = [
        pltpu.make_async_copy(x_ref.at[pl.ds(home, 2 * ROWS)], x_v.at[pl.ds(home, 2 * ROWS)], rest_sem.at[0]),
        pltpu.make_async_copy(gates_hbm, gates_ref, rest_sem.at[1]),
        pltpu.make_async_copy(sets_hbm, sets_ref, rest_sem.at[2]),
    ]

    def exchange(stage, chunk, partner):
        source = [send.at[0], send.at[1], send.at[2], recv.at[2], send.at[2], recv.at[4]][stage]
        target = [0, 1, 2, 3, 4, 3][stage]
        return pltpu.make_async_remote_copy(
            src_ref=source.at[chunk],
            dst_ref=recv.at[target, chunk],
            send_sem=send_sem.at[[0, 1, 2, 3, 2, 4][stage], chunk],
            recv_sem=recv_sem.at[target, chunk],
            device_id=partner,
            device_id_type=pl.DeviceIdType.MESH,
        )

    def read(base, chunk):
        start = base + chunk * 2 * STEP
        return [x_v[pl.ds(start + part, PAIRS, stride=4), :] for part in range(4)]

    load(0).start()

    def first(chunk):
        load(chunk).wait()
        put(send.at[0], chunk, scaled(read(away, chunk)))

    def send_first():
        exchange(0, 0, partner_f).start()
        for chunk in range(1, CHUNKS):
            load(chunk).start()
        for copy in rest:
            copy.start()

        @pl.loop(1, CHUNKS)
        def _(chunk):
            first(chunk)
            exchange(0, chunk, partner_f).start()

    def prepare():
        for copy in rest:
            copy.wait()
        spread_gate(0, own[0], own[1], gates_ref, sets_ref, weights)

        @pl.loop(0, CHUNKS)
        def _(chunk):
            put(kept.at[0], chunk, [part.astype(jnp.bfloat16) for part in read(home, chunk)])

        spread_gate(1, own[1], own[2], gates_ref, sets_ref, weights)
        spread_gate(2, own[2], None, gates_ref, sets_ref, weights)
        exchange(0, 0, core).wait_recv()

    first(0)

    @pl.when(lower)
    def _():
        pl.semaphore_wait(barrier, 2)

    @pl.when(jnp.logical_not(lower))
    def _():
        pl.semaphore_wait(barrier, 3)
        greet(ready_sem, partner_g)

    send_first()
    prepare()

    @pl.when(lower)
    def _():
        pl.semaphore_wait(ready_sem, 1)

    z_low = wide // (n_wide // 8)
    holds = z_low == 7
    held = jnp.where(holds, 1, 0)
    early_lower = EARLY + jnp.where(lax.rem(z_low, 4) == 3, 1, 0)
    early = jnp.where(lower, early_lower, EARLY)
    early_from_g = jnp.where(lower, EARLY, early_lower)

    def gate(layer, stage, chunk):
        block = jnp.concatenate([recv[stage, chunk], kept[layer, chunk]], axis=1)
        return jnp.dot(block, weights[layer], preferred_element_type=jnp.float32)

    def advance(layer, chunk, stage, partner, arrived=False):
        if not arrived:
            exchange(layer, chunk, core).wait_recv()
        result = gate(layer, layer, chunk)
        put(send.at[layer + 1], chunk, scaled(quarters(result[:, :256])))
        if stage == 4:
            pl.when(jnp.logical_not(holds))(exchange(4, chunk, partner_f).start)
        else:
            exchange(stage, chunk, partner).start()
        kept[layer + 1, chunk] = result[:, 256:].astype(jnp.bfloat16)

    advance(0, 0, 1, core, arrived=True)

    @pl.loop(1, early + 1)
    def _(chunk):
        advance(0, chunk, 1, core)
        advance(1, chunk - 1, 2, partner_g)

    @pl.loop(early + 1, CHUNKS)
    def _(chunk):
        advance(0, chunk, 1, core)
        advance(1, chunk - 1, 4, partner_f)

    advance(1, CHUNKS - 1, 4, partner_f)

    def relay_to_g(chunk):
        exchange(4, chunk, core).wait_recv()
        exchange(5, chunk, partner_g).start()

    @pl.when(holds)
    def _():
        relay_to_g(early)

        @pl.loop(early, CHUNKS)
        def _(chunk):
            exchange(4, chunk, partner_f).start()

    @pl.loop(0, early_from_g)
    def _(chunk):
        exchange(2, chunk, core).wait_recv()
        exchange(3, chunk, partner_f).start()

    @pl.loop(early + held, CHUNKS)
    def _(chunk):
        relay_to_g(chunk)

    @pl.loop(0, CHUNKS)
    def _(chunk):
        for stage in range(2):
            exchange(stage, chunk, core).wait_send()

    turn_from = jnp.where(jnp.logical_and(lower, z_low == 0), 0, early_from_g)

    @pl.loop(0, CHUNKS)
    def _(turn):
        chunk = lax.rem(turn + turn_from, CHUNKS)
        exchange(3, chunk, core).wait_recv()
        result = gate(2, 3, chunk)
        for half in range(2):
            start = half * 2 * ROWS + chunk * 2 * STEP
            for part, value in enumerate(quarters(result[:, half * 256 : half * 256 + 256])):
                out_ref[pl.ds(start + part, PAIRS, stride=4), :] = value

    @pl.loop(0, CHUNKS)
    def _(chunk):
        exchange(2, chunk, core).wait_send()

    @pl.loop(0, early_from_g)
    def _(chunk):
        exchange(3, chunk, core).wait_send()

    @pl.loop(early, CHUNKS)
    def _(chunk):
        exchange(5, chunk, core).wait_send()


def on_device(amplitudes, gates, qubit_sets):
    rows = amplitudes.reshape(2, 2 * ROWS, 128).transpose(1, 0, 2).reshape(4 * ROWS, 128)
    out = pl.pallas_call(
        kernel,
        out_shape=pltpu.VMEM((4 * ROWS, 128), jnp.float32),
        in_specs=[
            pl.BlockSpec(memory_space=pl.ANY),
            pl.BlockSpec(memory_space=pl.ANY),
            pl.BlockSpec(memory_space=pl.ANY),
        ],
        out_specs=pl.BlockSpec(memory_space=pltpu.VMEM),
        scratch_shapes=[
            pltpu.SMEM((LAYERS, 7), jnp.int32),
            pltpu.VMEM((LAYERS, 2, 128, 128), jnp.float32),
            pltpu.VMEM((4 * ROWS, 128), jnp.float32),
            pltpu.VMEM((LAYERS, 512, 512), jnp.bfloat16),
            pltpu.VMEM((3, CHUNKS, STEP, 256), jnp.bfloat16),
            pltpu.VMEM((5, CHUNKS, STEP, 256), jnp.bfloat16),
            pltpu.VMEM((3, CHUNKS, STEP, 256), jnp.bfloat16),
            pltpu.SemaphoreType.DMA((CHUNKS,)),
            pltpu.SemaphoreType.DMA((3,)),
            pltpu.SemaphoreType.DMA((5, CHUNKS)),
            pltpu.SemaphoreType.DMA((5, CHUNKS)),
            pltpu.SemaphoreType.REGULAR,
        ],
        compiler_params=pltpu.CompilerParams(
            collective_id=0, has_side_effects=True, vmem_limit_bytes=60 * 1024 * 1024
        ),
        name="layers",
    )(qubit_sets, gates, rows)
    return out.reshape(2 * ROWS, 2, 128).transpose(1, 0, 2).reshape(2, 2 * ROWS * 128)


def solution(mesh):
    in_specs = (P(None, ("wide", "mid", "narrow")), P(), P())
    out_specs = P(None, ("wide", "mid", "narrow"))
    return jax.shard_map(
        on_device, mesh=mesh, in_specs=in_specs, out_specs=out_specs, check_vma=False
    )
```
